128 devices in a mesh: band: 64 (over y_lo, z, x, core), feat: 2 (over y_hi).
Axes of the slice: x: 4, y: 4 (y_hi: 2, y_lo: 2; y = y_hi * 2 + y_lo), z: 4, core: 2. Of those that a mesh axis runs over, the one named last changes fastest.
Arguments:
- grid_feat: bfloat16 [131072, 1024], P('band'), may hold values from -6 to 6
- mesh_feat: bfloat16 [32768, 1024], P('band'), may hold values from -6 to 6
- edge_src: int32 [524288], P('band'), may hold values from 0 to 2047
- edge_dst: int32 [524288], P('band'), may hold values from 0 to 1535, as said below
- w_grid: bfloat16 [1024, 1024], P(None, 'feat'), may hold values from -0.1875 to 0.1875
- w_mesh: bfloat16 [1024, 1024], P(None, 'feat'), may hold values from -0.1875 to 0.1875
- b_edge: bfloat16 [1024], P('feat'), may hold values from -4 to 4
- w_enc_out: bfloat16 [1024, 1024], P('feat'), may hold values from -0.046875 to 0.046875
- b_enc: bfloat16 [1024], replicated, may hold values from -3 to 3
- ln_gain: bfloat16 [1024], replicated, may hold values from 0.25 to 1.75
- w_query: bfloat16 [1024, 1024], P(None, 'feat')
- w_key: bfloat16 [1024, 1024], P(None, 'feat')
- w_value: bfloat16 [1024, 1024], P(None, 'feat'), may hold values from -0.1875 to 0.1875
- w_out: bfloat16 [1024, 1024], P('feat'), may hold values from -0.75 to 0.75
- b_out: bfloat16 [1024], replicated, may hold values from -3 to 3
Outputs:
- mesh_out: bfloat16 [32768, 1024], P('band', 'feat')
The draws below stay inside these ranges and needn't reach their ends.
Inputs may be any that keep to these rules, and one draw needn't show every extreme that they name: Every edge's target lies in a band that exists: edges of band 0 have edge_dst of 512 or more, edges of the last band less than 1024.
All inputs are finite; a program needn't handle non-finite values.
Results may differ from the reference program's by a relative error of at most 0.0096.
The reference program's roundings to bfloat16 on the way count: a program that leaves them out, or rounds other values in their place, can miss the bound.
Values may be sent and summed in bfloat16 or wider, within the bound.
A program may use at most 128 MiB of HBM per device.

```python
import jax
import jax.numpy as jnp
from jax import lax

H = 1024
HEADS = 16
HEAD = 64
GRID_DEV = 2048
E_DEV = 8192
M_DEV = 512
BANDS = 64
GRID = 131072
MESH = 32768
EDGES = 524288
N_BAND = 64


def draw_w_query(key, part):
    key = jax.random.fold_in(key, 11)
    return (jax.random.normal(key, (H, H), jnp.float32) * 1.5 * H ** (-0.5)).astype(jnp.bfloat16)


def draw_w_key(key, part):
    key = jax.random.fold_in(key, 23)
    return (jax.random.normal(key, (H, H), jnp.float32) * 1.5 * H ** (-0.5)).astype(jnp.bfloat16)


def draw_edge_dst(key, part):
    key = jax.random.fold_in(key, 5)
    positions = jnp.arange(BANDS * E_DEV, dtype=jnp.int32)
    band_index = positions // E_DEV
    within = positions % E_DEV
    lowest = jnp.where(band_index == 0, M_DEV, 0).astype(jnp.int32)
    highest = jnp.where(band_index == BANDS - 1, 2 * M_DEV, 3 * M_DEV).astype(jnp.int32)
    drawn = jax.random.randint(key, (BANDS * E_DEV,), lowest, highest, jnp.int32)
    drawn = jnp.where(within == 0, lowest, drawn)
    drawn = jnp.where(within == 1, highest - 1, drawn)
    return drawn.astype(jnp.int32)


def touch_ends(values, stream_key, smallest, high):
    extent = values.shape
    spot = [jax.random.randint(jax.random.fold_in(stream_key, axis), (), 0, extent[axis]) for axis in range(len(extent))]
    values = values.at[tuple(spot)].set(smallest)
    longest = extent.index(max(extent))
    spot[longest] = (spot[longest] + 1) % extent[longest]
    return values.at[tuple(spot)].set(high)


def level_of(rng, extent, pieces, low, high):
    loudness = 1.0
    for position, blocks in pieces:
        heights = jax.random.uniform(jax.random.fold_in(jax.random.fold_in(rng, 6), position), (blocks,), jnp.float32, low / len(pieces), high / len(pieces))
        loudness = loudness * jnp.repeat(jnp.exp(heights), extent[position] // blocks).reshape((-1,) + (1,) * (len(extent) - 1 - position))
    return loudness


def bell_draw(rng, shape, deviation, bound, pieces=(), kind=jnp.bfloat16):
    values = jax.random.normal(rng, shape, jnp.float32) * deviation
    if len(pieces) > 0:
        values = level_of(rng, shape, pieces, -0.22, 0.18) * values
    return jnp.clip(values, min=-bound, max=bound).astype(kind)


def setup_inputs(seed: int = 0) -> dict:
    key_list = jax.random.split(jax.random.key(seed), 16)
    grid_feat = bell_draw(key_list[0], (GRID, H), 1.0, 6.0, ((0, 64),))
    mesh_feat = bell_draw(key_list[1], (MESH, H), 1.0, 6.0, ((0, 64),))
    edge_src = touch_ends(jax.random.randint(key_list[2], (EDGES,), 0, GRID_DEV), jax.random.fold_in(key_list[2], 1), 0, GRID_DEV - 1).astype(jnp.int32)
    edge_dst = draw_edge_dst(jax.random.fold_in(key_list[15], 71), 0)
    w_grid = bell_draw(key_list[4], (H, H), H ** -0.5, 0.1875, ((1, 2),))
    w_mesh = bell_draw(key_list[5], (H, H), H ** -0.5, 0.1875, ((1, 2),))
    b_edge = bell_draw(key_list[6], (H,), 1.0, 4.0, ((0, 2),))
    w_enc_out = bell_draw(key_list[7], (H, H), (16 * H) ** -0.5, 0.046875, ((0, 2),))
    b_enc = bell_draw(key_list[8], (H,), 0.5, 3.0)
    ln_gain = jnp.clip(1.0 + 0.15 * jax.random.normal(key_list[9], (H,), jnp.float32), 0.25, 1.75).astype(jnp.bfloat16)
    w_query = draw_w_query(jax.random.fold_in(key_list[15], 71), 0)
    w_key = draw_w_key(jax.random.fold_in(key_list[15], 71), 0)
    w_value = bell_draw(key_list[12], (H, H), H ** -0.5, 0.1875, ((1, 2),))
    w_out = bell_draw(key_list[13], (H, H), (H // 16) ** -0.5, 0.75, ((0, 2),))
    b_out = bell_draw(key_list[14], (H,), 0.5, 3.0)
    return dict(grid_feat=grid_feat, mesh_feat=mesh_feat, edge_src=edge_src, edge_dst=edge_dst, w_grid=w_grid, w_mesh=w_mesh, b_edge=b_edge, w_enc_out=w_enc_out, b_enc=b_enc, ln_gain=ln_gain, w_query=w_query, w_key=w_key, w_value=w_value, w_out=w_out, b_out=b_out)


def reference(grid_feat, mesh_feat, edge_src, edge_dst, w_grid, w_mesh, b_edge, w_enc_out, b_enc, ln_gain, w_query, w_key, w_value, w_out, b_out):
    mesh_proj = jnp.dot(mesh_feat, w_mesh, preferred_element_type=jnp.float32).astype(jnp.bfloat16)
    zero_rows = jnp.zeros((M_DEV, H), jnp.bfloat16)
    padded = jnp.concatenate([zero_rows, mesh_proj, zero_rows], axis=0)

    def encode(band_index):
        grid_rows = lax.dynamic_slice_in_dim(grid_feat, band_index * GRID_DEV, GRID_DEV, 0)
        sources = lax.dynamic_slice_in_dim(edge_src, band_index * E_DEV, E_DEV, 0)
        targets = lax.dynamic_slice_in_dim(edge_dst, band_index * E_DEV, E_DEV, 0)
        grid_proj = jnp.dot(grid_rows, w_grid, preferred_element_type=jnp.float32)
        window = lax.dynamic_slice_in_dim(padded, band_index * M_DEV, 3 * M_DEV, 0)
        edge_input = grid_proj[sources] + window[targets].astype(jnp.float32) + b_edge.astype(jnp.float32)
        hidden = lax.optimization_barrier(jax.nn.silu(edge_input).astype(jnp.bfloat16)).astype(jnp.float32)
        return jax.ops.segment_sum(hidden, targets, num_segments=3 * M_DEV)
    windows = lax.map(encode, jnp.arange(N_BAND, dtype=jnp.int32))
    zero_block = jnp.zeros((1, M_DEV, H), jnp.float32)
    from_above = jnp.concatenate([zero_block, windows[:-1, 2 * M_DEV:]], axis=0)
    from_below = jnp.concatenate([windows[1:, :M_DEV], zero_block], axis=0)
    aggregate = (windows[:, M_DEV:2 * M_DEV] + from_above + from_below).reshape(MESH, H)
    aggregate_b = aggregate.astype(jnp.bfloat16)
    latent = mesh_feat.astype(jnp.float32) + jnp.dot(aggregate_b, w_enc_out, preferred_element_type=jnp.float32) + b_enc.astype(jnp.float32)
    row_mean = lax.optimization_barrier(jnp.mean(latent, axis=1, keepdims=True))
    row_var = lax.optimization_barrier(jnp.mean((latent - row_mean) ** 2, axis=1, keepdims=True))
    normed = ((latent - row_mean) * lax.rsqrt(row_var + 1e-05) * ln_gain.astype(jnp.float32)).astype(jnp.bfloat16)
    query = (jnp.dot(normed, w_query, preferred_element_type=jnp.float32) * HEAD ** (-0.5)).astype(jnp.bfloat16)
    key_rows = jnp.dot(normed, w_key, preferred_element_type=jnp.float32).astype(jnp.bfloat16)
    value_rows = jnp.dot(normed, w_value, preferred_element_type=jnp.float32).astype(jnp.bfloat16)
    key_pad = jnp.concatenate([zero_rows, key_rows, zero_rows], axis=0)
    value_pad = jnp.concatenate([zero_rows, value_rows, zero_rows], axis=0)

    def attend(band_index):
        query_heads = lax.dynamic_slice_in_dim(query, band_index * M_DEV, M_DEV, 0).astype(jnp.float32).reshape(M_DEV, HEADS, HEAD)
        key_heads = lax.dynamic_slice_in_dim(key_pad, band_index * M_DEV, 3 * M_DEV, 0).astype(jnp.float32).reshape(3 * M_DEV, HEADS, HEAD)
        value_heads = lax.dynamic_slice_in_dim(value_pad, band_index * M_DEV, 3 * M_DEV, 0).astype(jnp.float32).reshape(3 * M_DEV, HEADS, HEAD)
        scores = jnp.einsum('qhd,khd->hqk', query_heads, key_heads)
        neighbour = band_index + jnp.arange(3 * M_DEV, dtype=jnp.int32) // M_DEV - 1
        usable = (neighbour >= 0) & (neighbour < N_BAND)
        scores = jnp.where(usable[None, None, :], scores, jnp.float32(-1e+30))
        row_max = lax.optimization_barrier(jnp.max(scores, axis=2, keepdims=True))
        weights = jnp.exp(scores - row_max)
        row_total = lax.optimization_barrier(jnp.sum(weights, axis=2, keepdims=True))
        attention = lax.optimization_barrier((weights / row_total).astype(jnp.bfloat16)).astype(jnp.float32)
        mixed_heads = jnp.einsum('hqk,khd->qhd', attention, value_heads)
        return mixed_heads.reshape(M_DEV, H).astype(jnp.bfloat16)
    attn = lax.map(attend, jnp.arange(N_BAND, dtype=jnp.int32)).reshape(MESH, H)
    mesh_out = latent + jnp.dot(attn, w_out, preferred_element_type=jnp.float32) + b_out.astype(jnp.float32)
    return mesh_out.astype(jnp.bfloat16)
```

```python
import jax
import jax.numpy as jnp
from jax import lax
from jax.sharding import PartitionSpec as P

HEAD = 64


def with_halo(block, sides, width):
    for axis, dim in sides:
        count = lax.axis_size(axis)
        forward = [(i, i + 1) for i in range(count - 1)]
        backward = [(target, source) for source, target in forward]
        low = lax.ppermute(
            lax.slice_in_dim(block, block.shape[dim] - width, None, axis=dim), axis, forward
        )
        high = lax.ppermute(lax.slice_in_dim(block, 0, width, axis=dim), axis, backward)
        block = jnp.concatenate([low, block, high], axis=dim)
    return block


def passed_along(value, axis, steps):
    count = lax.axis_size(axis)
    initial, last = (max(0, -steps), min(count, count - steps))
    return lax.ppermute(value, axis, [(source, source + steps) for source in range(initial, last)])


def swapped(value):
    return lax.ppermute(value, "feat", [(0, 1), (1, 0)])


def own_columns(array, start, count):
    return lax.dynamic_slice_in_dim(array, start, count, array.ndim - 1)


def body(
    grid_feat,
    mesh_feat,
    edge_src,
    edge_dst,
    w_grid,
    w_mesh,
    b_edge,
    w_enc_out,
    b_enc,
    ln_gain,
    w_query,
    w_key,
    w_value,
    w_out,
    b_out,
):
    mesh_rows = mesh_feat.shape[0]
    half_width = w_grid.shape[1]
    band_id = lax.axis_index("band")
    band_count = lax.axis_size("band")
    col_start = lax.axis_index("feat") * half_width
    enc_other = swapped(w_enc_out)
    out_other = swapped(own_columns(w_out, half_width - col_start, half_width))
    out_own = own_columns(w_out, col_start, half_width)
    grid_proj = jnp.dot(grid_feat, w_grid, preferred_element_type=jnp.float32)
    mesh_proj = jnp.dot(mesh_feat, w_mesh, preferred_element_type=jnp.float32).astype(jnp.bfloat16)
    window = with_halo(mesh_proj, (("band", 0),), mesh_rows)
    edge_input = (
        grid_proj[edge_src] + window[edge_dst].astype(jnp.float32) + b_edge.astype(jnp.float32)
    )
    hidden = jax.nn.silu(edge_input).astype(jnp.bfloat16)
    targets = jnp.arange(3 * mesh_rows, dtype=jnp.int32)
    onehot = (targets[:, None] == edge_dst[None, :]).astype(jnp.bfloat16)
    partial_value = jnp.dot(onehot, hidden, preferred_element_type=jnp.float32)
    from_above = passed_along(partial_value[2 * mesh_rows :], "band", 1)
    from_below = passed_along(partial_value[:mesh_rows], "band", -1)
    aggregate = partial_value[mesh_rows : 2 * mesh_rows] + from_above + from_below
    own_half = aggregate.astype(jnp.bfloat16)
    other_half = swapped(own_half)
    summed = jnp.dot(own_half, w_enc_out, preferred_element_type=jnp.float32) + jnp.dot(
        other_half, enc_other, preferred_element_type=jnp.float32
    )
    latent = mesh_feat.astype(jnp.float32) + summed + b_enc.astype(jnp.float32)
    row_mean = jnp.mean(latent, axis=1, keepdims=True)
    row_var = jnp.mean((latent - row_mean) ** 2, axis=1, keepdims=True)
    normed = (
        (latent - row_mean) * lax.rsqrt(row_var + 1e-05) * ln_gain.astype(jnp.float32)
    ).astype(jnp.bfloat16)
    latent_half = own_columns(latent, col_start, half_width)
    query = (jnp.dot(normed, w_query, preferred_element_type=jnp.float32) * HEAD ** (-0.5)).astype(
        jnp.bfloat16
    )
    key_rows = jnp.dot(normed, w_key, preferred_element_type=jnp.float32).astype(jnp.bfloat16)
    value_rows = jnp.dot(normed, w_value, preferred_element_type=jnp.float32).astype(jnp.bfloat16)
    paired = jnp.concatenate([key_rows, value_rows], axis=1)
    key_window = with_halo(paired, (("band", 0),), mesh_rows)
    heads_here = half_width // HEAD
    query_heads = query.reshape(mesh_rows, heads_here, HEAD)
    key_heads = key_window[:, :half_width].reshape(3 * mesh_rows, heads_here, HEAD)
    value_heads = key_window[:, half_width:].reshape(3 * mesh_rows, heads_here, HEAD)
    scores = jnp.einsum("qhd,khd->hqk", query_heads, key_heads, preferred_element_type=jnp.float32)
    neighbour = band_id + targets // mesh_rows - 1
    usable = (neighbour >= 0) & (neighbour < band_count)
    scores = jnp.where(usable[None, None, :], scores, jnp.float32(-1e30))
    row_max = jnp.max(scores, axis=2, keepdims=True)
    weights = jnp.exp(scores - row_max)
    row_total = jnp.sum(weights, axis=2, keepdims=True)
    attention = (weights / row_total).astype(jnp.bfloat16)
    mixed_heads = jnp.einsum(
        "hqk,khd->qhd", attention, value_heads, preferred_element_type=jnp.float32
    )
    mixed_heads = mixed_heads.reshape(mesh_rows, half_width).astype(jnp.bfloat16)
    out_part = jnp.dot(mixed_heads, out_own, preferred_element_type=jnp.float32) + jnp.dot(
        swapped(mixed_heads), out_other, preferred_element_type=jnp.float32
    )
    result = latent_half + out_part + own_columns(b_out, col_start, half_width).astype(jnp.float32)
    return result.astype(jnp.bfloat16)


def solution(mesh):
    placed = (
        P("band", None),
        P("band", None),
        P("band"),
        P("band"),
        P(None, "feat"),
        P(None, "feat"),
        P("feat"),
        P("feat", None),
        P(),
        P(),
        P(None, "feat"),
        P(None, "feat"),
        P(None, "feat"),
        P("feat", None),
        P(),
    )
    return jax.shard_map(
        body, mesh=mesh, in_specs=placed, out_specs=P("band", "feat"), check_vma=False
    )
```
